1024 devices in a mesh: slab: 32 (over z), grp: 32 (over y, x, core).
Axes of the slice: x: 4, y: 4, z: 32, core: 2. Of those that a mesh axis runs over, the one named last changes fastest.
Arguments:
- multipoles: bfloat16 [32, 32768, 128], P('grp', 'slab'), may hold values from -6 to 6
- translations: float32 [16, 128, 128], replicated, may hold values from -0.5 to 0.5
- m2l_list: int32 [3, 32, 131072], P(None, 'grp', 'slab'), may hold values from 0 to 1023, as said below
- send_counts: int32 [32, 1024], P('grp', 'slab'), may hold values from 1 to 128, as said below
- positions: float32 [32, 3, 16384], P('grp', None, 'slab'), may hold values from 0 to 1
- charges: float32 [32, 16384], P('grp', 'slab'), may hold values from -0.3 to 0.3
- leaf_counts: int32 [32, 32], P('grp', 'slab'), may hold values from 64 to 512, as said below
- particle_cell: int32 [32, 16384], P('grp', 'slab'), may hold values from 0 to 1023
- basis: bfloat16 [32, 128, 16384], P('grp', None, 'slab'), may hold values from -0.1875 to 0.1875
Outputs:
- local_exp: float32 [32, 32768, 128], P('grp', 'slab')
- potential: float32 [32, 16384], P('grp', 'slab')
The draws below stay inside these ranges and needn't reach their ends.
Inputs may be any that keep to these rules, and one draw needn't show every extreme that they name: `m2l_list`: slot k * 128 + j of a device holds an entry for the peer at slab index k of its group: row 0 a target cell among the device's own 1024 cells, row 1 a source cell among that peer's 1024 cells, row 2 an offset id below 16. Only slots with j below the matching send count are read. `send_counts`: entry k of a device counts the rows that the peer at slab index k of its group sends to it (its used slots for that peer). In every group one device sends 128 rows to every device of the group, and every device receives 128 rows from some peer. `leaf_counts`: some device holds 512 live particles.
All inputs are finite; a program needn't handle non-finite values.
Results may differ from the reference program's by a relative error of at most 0.0003.
Values may be sent and summed in bfloat16 or wider, within the bound.
No kernel may reach another device: no remote copies, remote signals or barrier semaphores. Data moves between devices by JAX's collectives and lax.ppermute only.
A program may use at most 64 MiB of HBM per device.

```python
import jax
import jax.numpy as jnp
from jax import lax

P_SIZE = 128
OFFS = 16
CELLS_DEV = 1024
CAP = 128
PART_DEV = 512
GROUPS = 32
GCELLS = 32768
GSLOTS = 131072
GPARTS = 16384
N_SLAB = 32


def draw_m2l_list(key, part):
    key = jax.random.fold_in(key, 2)
    keys = jax.random.split(key, 3)
    target = jax.random.randint(keys[0], (GROUPS, GSLOTS), 0, CELLS_DEV)
    source = jax.random.randint(keys[1], (GROUPS, GSLOTS), 0, CELLS_DEV)
    offset = jax.random.randint(keys[2], (GROUPS, GSLOTS), 0, OFFS)
    return jnp.stack([target, source, offset]).astype(jnp.int32)


def draw_send_counts(key, part):
    key = jax.random.fold_in(key, 1)
    keys = jax.random.split(key, 3)
    counts = jax.random.randint(keys[0], (GROUPS, N_SLAB, N_SLAB), 1, CAP + 1)
    busy = jax.random.randint(keys[1], (GROUPS,), 0, N_SLAB)
    peers = jnp.arange(N_SLAB, dtype=jnp.int32)
    counts = jnp.where(peers[None, None, :] == busy[:, None, None], CAP, counts)
    chosen = jax.random.randint(keys[2], (GROUPS, N_SLAB), 0, N_SLAB)
    counts = jnp.where(peers[None, None, :] == chosen[:, :, None], CAP, counts)
    return counts.reshape(GROUPS, N_SLAB * N_SLAB).astype(jnp.int32)


def draw_leaf_counts(key, part):
    key = jax.random.fold_in(key, 3)
    keys = jax.random.split(key, 2)
    counts = jax.random.randint(keys[0], (GROUPS, N_SLAB), PART_DEV // 8, PART_DEV // 3 + 1)
    full = jax.random.randint(keys[1], (), 0, GROUPS * N_SLAB)
    flat = jnp.arange(GROUPS * N_SLAB, dtype=jnp.int32).reshape(GROUPS, N_SLAB)
    return jnp.where(flat == full, PART_DEV, counts).astype(jnp.int32)


def set_ends(array, own_key, low, top_value):
    longest = array.shape.index(max(array.shape))
    spots = []
    for shift in (0, 1):
        where = [jax.random.randint(jax.random.fold_in(own_key, axis), (), 0, length) for axis, length in enumerate(array.shape)]
        where[longest] = (where[longest] + shift) % array.shape[longest]
        spots.append(tuple(where))
    return array.at[spots[0]].set(low).at[spots[1]].set(top_value)


def block_scale(key, dims, pieces, low, largest):
    def one(dim, blocks):
        steps = jax.random.uniform(jax.random.fold_in(jax.random.fold_in(key, 6), dim), (blocks,), jnp.float32, low / len(pieces), largest / len(pieces))
        return jnp.repeat(jnp.exp(steps), dims[dim] // blocks).reshape((-1,) + (1,) * (len(dims) - dim - 1))

    factor_of = one(*pieces[0])
    for cut in pieces[1:]:
        factor_of = factor_of * one(*cut)
    return factor_of


def gaussian(stream_key, dims, width, most, shards=(), kind=jnp.bfloat16):
    factor_of = block_scale(stream_key, dims, shards, -0.22, 0.18) if shards else 1.0
    result = jax.random.normal(stream_key, dims, jnp.float32) * width * factor_of
    return jnp.minimum(jnp.maximum(result, -most), most).astype(kind)


def setup_inputs(seed: int = 0) -> dict:
    arg_keys = jax.random.split(jax.random.key(seed), 10)
    multipoles = gaussian(arg_keys[0], (GROUPS, GCELLS, P_SIZE), 1.0, 6.0, ((0, 32), (1, 32)))
    translations = gaussian(arg_keys[1], (OFFS, P_SIZE, P_SIZE), P_SIZE ** -0.5, 0.5, (), jnp.float32)
    m2l_list = draw_m2l_list(jax.random.fold_in(arg_keys[9], 71), 0)
    send_counts = draw_send_counts(jax.random.fold_in(arg_keys[9], 71), 0)
    positions = jnp.clip(1.0 * jax.random.uniform(arg_keys[4], (GROUPS, 3, GPARTS), jnp.float32) ** block_scale(arg_keys[4], (GROUPS, 3, GPARTS), ((0, 32), (2, 32)), -0.2, 0.2), 0.0, 1.0)
    charges = gaussian(arg_keys[5], (GROUPS, GPARTS), 0.05, 0.3, ((0, 32), (1, 32)), jnp.float32)
    leaf_counts = draw_leaf_counts(jax.random.fold_in(arg_keys[9], 71), 0)
    particle_cell = set_ends(jax.random.randint(arg_keys[7], (GROUPS, GPARTS), 0, CELLS_DEV), jax.random.fold_in(arg_keys[7], 1), 0, CELLS_DEV - 1).astype(jnp.int32)
    basis = gaussian(arg_keys[8], (GROUPS, P_SIZE, GPARTS), (8 * P_SIZE) ** -0.5, 0.1875, ((0, 32), (2, 32)))
    return {"multipoles": multipoles, "translations": translations, "m2l_list": m2l_list, "send_counts": send_counts, "positions": positions, "charges": charges, "leaf_counts": leaf_counts, "particle_cell": particle_cell, "basis": basis}


SOFT = 0.01

def pair_sum(targets, sources, weights):
    dist = (targets[0][:, None] - sources[0][None, :]) ** 2
    dist = dist + (targets[1][:, None] - sources[1][None, :]) ** 2
    dist = dist + (targets[2][:, None] - sources[2][None, :]) ** 2
    return lax.optimization_barrier(jnp.sum(weights[None, :] / jnp.sqrt(dist + SOFT), axis=1))

def reference(multipoles, translations, m2l_list, send_counts, positions, charges, leaf_counts, particle_cell, basis):
    slot_index = jnp.arange(GPARTS, dtype=jnp.int32) % PART_DEV
    live = slot_index[None, :] < jnp.repeat(leaf_counts, PART_DEV, axis=1)
    masked = jnp.where(live, charges, 0.0).astype(jnp.float32)
    grid_pos = positions.reshape(GROUPS, 3, N_SLAB, PART_DEV)
    grid_q = masked.reshape(GROUPS, N_SLAB, PART_DEV)
    pad_pos = jnp.pad(grid_pos, ((1, 1), (0, 0), (0, 0), (0, 0)))
    pad_q = jnp.pad(grid_q, ((1, 1), (0, 0), (0, 0)))
    paired = jax.vmap(pair_sum, in_axes=(1, 1, 0))

    def near_one(group):
        targets = grid_pos[group]
        total = jnp.zeros((N_SLAB, PART_DEV), jnp.float32)
        for shift_k in range(3):
            sources = lax.dynamic_index_in_dim(pad_pos, group + shift_k, 0, keepdims=False)
            weights = lax.dynamic_index_in_dim(pad_q, group + shift_k, 0, keepdims=False)
            total = total + paired(targets, sources, weights)
        return total.reshape(GPARTS)
    groups = jnp.arange(GROUPS, dtype=jnp.int32)
    near = lax.map(near_one, groups)
    flat_trans = translations.reshape(OFFS * P_SIZE, P_SIZE)
    owner_ids = jnp.arange(N_SLAB, dtype=jnp.int32)
    slot_ids = jnp.arange(CAP, dtype=jnp.int32)
    device_of = jnp.arange(GPARTS, dtype=jnp.int32) // PART_DEV

    def far_one(group):
        rows_all = multipoles[group].astype(jnp.float32)
        entries = m2l_list[:, group].reshape(3, N_SLAB, N_SLAB, CAP)
        counts = send_counts[group].reshape(N_SLAB, N_SLAB)
        valid = slot_ids[None, None, :] < counts[:, :, None]
        source = owner_ids[None, :, None] * CELLS_DEV + entries[1]
        rows = rows_all[source] * valid[..., None].astype(jnp.float32)
        segment = (owner_ids[:, None, None] * CELLS_DEV + entries[0]) * OFFS + entries[2]
        summed = jax.ops.segment_sum(rows.reshape(-1, P_SIZE), segment.reshape(-1), num_segments=GCELLS * OFFS)
        local = jnp.dot(summed.reshape(GCELLS, OFFS * P_SIZE), flat_trans, precision=lax.Precision.HIGHEST, preferred_element_type=jnp.float32)
        cell_rows = local[device_of * CELLS_DEV + particle_cell[group]]
        far = lax.optimization_barrier(jnp.sum(cell_rows.T * basis[group].astype(jnp.float32), axis=0))
        return (local, far)
    local_exp, far = lax.map(far_one, groups)
    potential = jnp.where(live, near + far, 0.0).astype(jnp.float32)
    return (local_exp, potential)
```

```python
import functools

import jax
import jax.numpy as jnp
from jax import lax
from jax.experimental import pallas as pl
from jax.experimental.pallas import tpu as pltpu
from jax.sharding import PartitionSpec as P

SOFT = 0.01
SLABS = 32
STRIDE = 4
EARLY = (0, 1, -1, 2, -2)
LATE = (3, -3, 4)
ORDER = EARLY + LATE
RELAYED = {1: ORDER, -1: ORDER, 2: (0, 1, 2, 3), -2: (0, -1, -2, -3)}
VMEM_BYTES = 56 * 1024 * 1024


def shifted(value, amount):
    count = lax.axis_size("slab")
    pairs = [(i, (i + amount) % count) for i in range(count)]
    return lax.ppermute(value, "slab", pairs)


def ask_kernel(me_ref, list_ref, *outs):
    for out, (relay, ks) in zip(outs, RELAYED.items(), strict=True):
        for i, k in enumerate(ks):
            out[pl.ds(i, 1), :] = list_ref[1, pl.ds(peer(me_ref[0], relay, k), 1), :]


def peer(me, relay, k):
    return lax.rem(me + (relay + STRIDE * k + SLABS), SLABS)


def ask(me, lists):
    return pl.pallas_call(
        ask_kernel,
        out_shape=[jax.ShapeDtypeStruct((len(ks), lists.shape[2]), jnp.int32) for ks in RELAYED.values()],
        in_specs=[pl.BlockSpec(memory_space=pltpu.SMEM), pl.BlockSpec(memory_space=pltpu.VMEM)],
        out_specs=[pl.BlockSpec(memory_space=pltpu.VMEM)] * len(RELAYED),
    )(me, lists)


def table_kernel(matrix_ref, out_ref):
    for o in range(matrix_ref.shape[0]):
        turned = matrix_ref[o].T
        high = turned.astype(jnp.bfloat16)
        out_ref[0:128, o * 128 : (o + 1) * 128] = high
        rest = turned - high.astype(jnp.float32)
        out_ref[128:256, o * 128 : (o + 1) * 128] = rest.astype(jnp.bfloat16)


def split_table(translations):
    return pl.pallas_call(
        table_kernel,
        out_shape=jax.ShapeDtypeStruct((256, translations.shape[0] * 128), jnp.bfloat16),
        in_specs=[pl.BlockSpec(memory_space=pltpu.VMEM)],
        out_specs=pl.BlockSpec(memory_space=pltpu.VMEM),
        compiler_params=pltpu.CompilerParams(vmem_limit_bytes=VMEM_BYTES),
    )(translations)


def pack_kernel(plan, half, carried, me_ref, list_ref, *refs):
    asked = dict(zip(RELAYED, refs[: len(RELAYED)], strict=True))
    refs = refs[len(RELAYED) :]
    for i in range(carried):
        refs[carried + 2 * len(plan) + 1 + i][0 : refs[i].shape[0]] = refs[i][...]
    blocks = refs[carried : carried + 2 * len(plan)]
    outs = refs[carried + 2 * len(plan) :]
    for b, (k, uses) in enumerate(plan):
        lists = []
        for relay, _, _ in uses:
            if relay == 0:
                lists.append(list_ref[1, pl.ds(peer(me_ref[0], 0, k), 1), :])
            else:
                lists.append(asked[relay][pl.ds(RELAYED[relay].index(k), 1), :])
        wanted = jnp.concatenate(lists, axis=1)
        total = None
        for h in range(2):
            place = lax.broadcasted_iota(jnp.int32, (half, wanted.shape[1]), 0)
            pick = jnp.where(place + h * half == wanted, 1.0, 0.0).astype(jnp.bfloat16)
            part = lax.dot_general(
                blocks[2 * b + h][...],
                pick,
                (((0,), (0,)), ((), ())),
                preferred_element_type=jnp.float32,
            )
            total = part if total is None else total + part
        rows = total.astype(jnp.bfloat16)
        for i, (_, dest, slot) in enumerate(uses):
            outs[dest][slot] = rows[:, i * 128 : (i + 1) * 128]


def pack(names, blocks, me, lists, asked, before=None):
    relays = [0, *RELAYED]
    carried = [] if before is None else [before[relay] for relay in RELAYED]
    sizes = dict.fromkeys(relays, 0)
    for relay, part in zip(RELAYED, carried, strict=False):
        sizes[relay] = part.shape[0]
    plan = []
    for k in names:
        uses = []
        for dest, relay in enumerate(relays):
            if relay == 0 or k in RELAYED[relay]:
                uses.append((relay, dest, sizes[relay]))
                sizes[relay] += 1
        plan.append((k, uses))
    flat = [half for k in names for half in blocks[k]]
    rows = sum(len(uses) for _, uses in plan) * 128
    outs = pl.pallas_call(
        functools.partial(pack_kernel, plan, flat[0].shape[0], len(carried)),
        out_shape=[jax.ShapeDtypeStruct((sizes[r], 128, 128), jnp.bfloat16) for r in relays],
        in_specs=[pl.BlockSpec(memory_space=pltpu.SMEM)]
        + [pl.BlockSpec(memory_space=pltpu.VMEM)] * (1 + len(RELAYED) + len(carried) + len(flat)),
        out_specs=[pl.BlockSpec(memory_space=pltpu.VMEM)] * len(relays),
        compiler_params=pltpu.CompilerParams(vmem_limit_bytes=VMEM_BYTES),
        cost_estimate=pl.CostEstimate(
            flops=2 * rows * 1024 * 128, bytes_accessed=len(flat) * 131072, transcendentals=0
        ),
    )(me, lists, *asked, *carried, *flat)
    return dict(zip(relays, outs, strict=True))


def translate_kernel(groups, cells, me_ref, count_ref, table_ref, list_ref, start_ref, *refs):
    rows, out_ref, total = refs[:-2], refs[-2], refs[-1]
    offsets = table_ref.shape[1] // 128
    lane = lax.broadcasted_iota(jnp.int32, (1, 128), 1)
    for n, group in enumerate(groups):
        taken = jnp.concatenate([rows[a][b] for a, b, _, _ in group], axis=1)
        targets, kinds = [], []
        for _, _, relay, k in group:
            at = peer(me_ref[0], relay, k)
            targets.append(list_ref[0, pl.ds(at, 1), :])
            kinds.append(jnp.where(lane < count_ref[at], list_ref[2, pl.ds(at, 1), :], -1))
        target = jnp.concatenate(targets, axis=1)
        kind = jnp.concatenate(kinds, axis=1)
        spread = jnp.concatenate(
            [taken * jnp.where(kind == o, 1.0, 0.0).astype(jnp.bfloat16) for o in range(offsets)],
            axis=0,
        )
        both = jnp.dot(table_ref[...], spread, preferred_element_type=jnp.float32)
        moved = both[:128] + both[128:]
        high = moved.astype(jnp.bfloat16)
        low = (moved - high.astype(jnp.float32)).astype(jnp.bfloat16)
        place = lax.broadcasted_iota(jnp.int32, (cells, target.shape[1]), 0)
        pick = jnp.where(place == target, 1.0, 0.0).astype(jnp.bfloat16)
        part = lax.dot_general(
            pick,
            jnp.concatenate([high, low], axis=0),
            (((1,), (1,)), ((), ())),
            preferred_element_type=jnp.float32,
        )
        if n == 0:
            total[...] = part
        else:
            total[...] += part
    out = total[:, :128] + total[:, 128:]
    out_ref[...] = out if start_ref is None else start_ref[...] + out


def translate(me, counts, table, lists, start, parts, cells):
    flat = [(a, b, relay, k) for a, (_, relay, ks) in enumerate(parts) for b, k in enumerate(ks)]
    groups = [flat[i : i + 4] for i in range(0, len(flat), 4)]
    given = [] if start is None else [start]

    def body(me_ref, count_ref, table_ref, list_ref, *refs):
        first = refs[0] if given else None
        translate_kernel(groups, cells, me_ref, count_ref, table_ref, list_ref, first, *refs[len(given) :])

    return pl.pallas_call(
        body,
        out_shape=jax.ShapeDtypeStruct((cells, 128), jnp.float32),
        in_specs=[pl.BlockSpec(memory_space=pltpu.SMEM)] * 2
        + [pl.BlockSpec(memory_space=pltpu.VMEM)] * (2 + len(given) + len(parts)),
        out_specs=pl.BlockSpec(memory_space=pltpu.VMEM),
        scratch_shapes=[pltpu.VMEM((cells, 256), jnp.float32)],
        compiler_params=pltpu.CompilerParams(vmem_limit_bytes=VMEM_BYTES),
        cost_estimate=pl.CostEstimate(
            flops=2 * len(flat) * 128 * 256 * (table.shape[1] + cells),
            bytes_accessed=len(flat) * 32768 + 2 * cells * 512,
            transcendentals=0,
        ),
    )(me, counts, table, lists, *given, *[part for part, _, _ in parts])


def extended(block, axis):
    count = lax.axis_size(axis)
    forward = [(i, i + 1) for i in range(count - 1)]
    backward = [(target, source) for source, target in forward]
    return [lax.ppermute(block, axis, forward), block, lax.ppermute(block, axis, backward)]


def pair_sum(targets, sources):
    dist = (targets[0][:, None] - sources[0][None, :]) ** 2
    dist = dist + (targets[1][:, None] - sources[1][None, :]) ** 2
    dist = dist + (targets[2][:, None] - sources[2][None, :]) ** 2
    return jnp.sum(sources[3][None, :] / jnp.sqrt(dist + SOFT), axis=1)


def shards(
    multipoles,
    translations,
    m2l_list,
    send_counts,
    positions,
    charges,
    leaf_counts,
    particle_cell,
    basis,
):
    cells_dev = multipoles.shape[1]
    part_dev = charges.shape[1]
    me = lax.axis_index("slab").astype(jnp.int32).reshape(1)
    lists = m2l_list.reshape(3, SLABS, m2l_list.shape[2] // SLABS)
    counts = send_counts[0]

    asked = [shifted(value, relay) for value, relay in zip(ask(me, lists), RELAYED, strict=True)]
    half = cells_dev // 2
    own, asked = lax.optimization_barrier(
        ((multipoles[0, :half], multipoles[0, half:]), asked)
    )

    blocks = {0: own}
    for k in (1, 2, 3, 4):
        up, down = blocks[1 - k], blocks[k - 1]
        if k == 2:
            _, positions, translations = lax.optimization_barrier(
                (up[0], positions, translations)
            )
        if k == 4:
            table = split_table(translations)
            first = pack(EARLY, blocks, me, lists, asked)
            local = translate(me, counts, table, lists, None, [(first[0], 0, EARLY)], cells_dev)
            low, high, local = lax.optimization_barrier((up[0], down[1], local))
            blocks[4] = (shifted(low, STRIDE), shifted(high, -STRIDE))
        else:
            blocks[-k] = tuple(shifted(part, STRIDE) for part in up)
            blocks[k] = tuple(shifted(part, -STRIDE) for part in down)

    second = pack(LATE, blocks, me, lists, asked, first)
    arrived = {relay: shifted(second[relay], -relay) for relay in RELAYED}
    parts = [(arrived[r], r, [k for k in ORDER if k in RELAYED[r]]) for r in RELAYED]
    parts = [(second[0], 0, LATE), *parts]
    local = translate(me, counts, table, lists, local, parts, cells_dev)

    live = jnp.arange(part_dev, dtype=jnp.int32) < leaf_counts[0, 0]
    masked = jnp.where(live, charges[0], 0.0)
    stacked = jnp.concatenate([positions[0], masked[None, :]], axis=0)
    near = sum(pair_sum(positions[0], sources) for sources in extended(stacked, "grp"))
    cell_rows = local[particle_cell[0]]
    far = jnp.sum(cell_rows.T * basis[0].astype(jnp.float32), axis=0)
    potential = jnp.where(live, near + far, 0.0)
    return (local[None], potential[None])


def solution(mesh):
    placed = (
        P("grp", "slab", None),
        P(),
        P(None, "grp", "slab"),
        P("grp", "slab"),
        P("grp", None, "slab"),
        P("grp", "slab"),
        P("grp", "slab"),
        P("grp", "slab"),
        P("grp", None, "slab"),
    )
    return jax.shard_map(
        shards,
        mesh=mesh,
        in_specs=placed,
        out_specs=(P("grp", "slab", None), P("grp", "slab")),
        check_vma=False,
    )
```

```python
import functools

import jax
import jax.numpy as jnp
from jax import lax
from jax.experimental import pallas as pl
from jax.experimental.pallas import tpu as pltpu
from jax.sharding import PartitionSpec as P

SOFT = 0.01
SLABS = 32
STRIDE = 4
GATHERED = 16
EARLY = (0, 1, -1, 2, -2)
ORDER = (*EARLY, 3, -3, 4)
RELAYED = {1: ORDER, -1: ORDER, 2: (0, 1, 2, 3), -2: (0, -1, -2, -3)}
VMEM_BYTES = 56 * 1024 * 1024


def shifted(value, amount):
    count = lax.axis_size("slab")
    pairs = [(i, (i + amount) % count) for i in range(count)]
    return lax.ppermute(value, "slab", pairs)


def ask_kernel(me_ref, list_ref, *outs):
    for out, (relay, ks) in zip(outs, RELAYED.items(), strict=True):
        for i, k in enumerate(ks):
            out[pl.ds(i, 1), :] = list_ref[1, pl.ds(peer(me_ref[0], relay, k), 1), :]


def peer(me, relay, k):
    return lax.rem(me + (relay + STRIDE * k + SLABS), SLABS)


def ask(me, lists):
    return pl.pallas_call(
        ask_kernel,
        out_shape=[jax.ShapeDtypeStruct((len(ks), lists.shape[2]), jnp.int32) for ks in RELAYED.values()],
        in_specs=[pl.BlockSpec(memory_space=pltpu.SMEM), pl.BlockSpec(memory_space=pltpu.VMEM)],
        out_specs=[pl.BlockSpec(memory_space=pltpu.VMEM)] * len(RELAYED),
    )(me, lists)


def table_kernel(matrix_ref, out_ref):
    for o in range(matrix_ref.shape[0]):
        turned = matrix_ref[o].T
        high = turned.astype(jnp.bfloat16)
        out_ref[0:128, o * 128 : (o + 1) * 128] = high
        rest = turned - high.astype(jnp.float32)
        out_ref[128:256, o * 128 : (o + 1) * 128] = rest.astype(jnp.bfloat16)


def split_table(translations):
    return pl.pallas_call(
        table_kernel,
        out_shape=jax.ShapeDtypeStruct((256, translations.shape[0] * 128), jnp.bfloat16),
        in_specs=[pl.BlockSpec(memory_space=pltpu.VMEM)],
        out_specs=pl.BlockSpec(memory_space=pltpu.VMEM),
        compiler_params=pltpu.CompilerParams(vmem_limit_bytes=VMEM_BYTES),
    )(translations)


def pack_kernel(plan, known, me_ref, list_ref, *refs):
    asked = dict(zip(RELAYED, refs[: len(RELAYED)], strict=True))
    refs = refs[len(RELAYED) :]
    count = len(RELAYED) + 1
    before = refs[:count] if known else ()
    blocks, outs = refs[len(before) : -count], refs[-count:]
    for k, parts, uses in plan:
        lists = []
        for relay, _ in uses:
            if relay == 0:
                lists.append(list_ref[1, pl.ds(peer(me_ref[0], 0, k), 1), :])
            else:
                lists.append(asked[relay][pl.ds(RELAYED[relay].index(k), 1), :])
        wanted = jnp.concatenate(lists, axis=1)
        total = None
        for ref, turn, base in parts:
            if turn:
                count_groups = blocks[ref].shape[0]
                block = blocks[ref][lax.rem(me_ref[0] // STRIDE + (k + count_groups), count_groups)]
            else:
                block = blocks[ref][...]
            place = lax.broadcasted_iota(jnp.int32, (block.shape[0], wanted.shape[1]), 0)
            pick = jnp.where(place + base == wanted, 1.0, 0.0).astype(jnp.bfloat16)
            part = lax.dot_general(
                block, pick, (((0,), (0,)), ((), ())), preferred_element_type=jnp.float32
            )
            total = part if total is None else total + part
        rows = total.astype(jnp.bfloat16)
        for i, (relay, slot) in enumerate(uses):
            dest = 0 if relay == 0 else 1 + list(RELAYED).index(relay)
            row = rows[:, i * 128 : (i + 1) * 128]
            if k in known:
                row = row + before[dest][kept(known, relay).index(k)]
            outs[dest][slot] = row


def kept(names, relay):
    return [k for k in names if relay == 0 or k in RELAYED[relay]]


def pack(parts, blocks, me, lists, asked, known=(), before=()):
    relays = [0, *RELAYED]
    plan = []
    for k in parts:
        uses = [(r, kept(parts, r).index(k)) for r in relays if r == 0 or k in RELAYED[r]]
        plan.append((k, parts[k], uses))
    sizes = [len(kept(parts, r)) for r in relays]
    return pl.pallas_call(
        functools.partial(pack_kernel, plan, known),
        out_shape=[jax.ShapeDtypeStruct((size, 128, 128), jnp.bfloat16) for size in sizes],
        in_specs=[pl.BlockSpec(memory_space=pltpu.SMEM)]
        + [pl.BlockSpec(memory_space=pltpu.VMEM)] * (1 + len(asked) + len(before) + len(blocks)),
        out_specs=[pl.BlockSpec(memory_space=pltpu.VMEM)] * len(sizes),
        compiler_params=pltpu.CompilerParams(vmem_limit_bytes=VMEM_BYTES),
        cost_estimate=pl.CostEstimate(
            flops=2 * 4096 * 512 * 128, bytes_accessed=2 * 1024 * 1024, transcendentals=0
        ),
    )(me, lists, *asked, *before, *blocks)


def translate_kernel(groups, me_ref, count_ref, live_ref, table_ref, list_ref, near_ref, cell_ref, basis_ref, *refs):
    rows, out_ref, potential_ref, total = refs[:-3], refs[-3], refs[-2], refs[-1]
    cells, slots = out_ref.shape[1], near_ref.shape[1]
    offsets = table_ref.shape[1] // 128
    lane = lax.broadcasted_iota(jnp.int32, (1, 128), 1)
    for n, group in enumerate(groups):
        taken = jnp.concatenate([rows[a][b] for a, b, _, _ in group], axis=1)
        targets, kinds = [], []
        for _, _, relay, k in group:
            at = peer(me_ref[0], relay, k)
            targets.append(list_ref[0, pl.ds(at, 1), :])
            kinds.append(jnp.where(lane < count_ref[at], list_ref[2, pl.ds(at, 1), :], -1))
        target = jnp.concatenate(targets, axis=1)
        kind = jnp.concatenate(kinds, axis=1)
        spread = jnp.concatenate(
            [taken * jnp.where(kind == o, 1.0, 0.0).astype(jnp.bfloat16) for o in range(offsets)],
            axis=0,
        )
        both = jnp.dot(table_ref[...], spread, preferred_element_type=jnp.float32)
        pair = split(both[:128] + both[128:], 0)
        place = lax.broadcasted_iota(jnp.int32, (cells, target.shape[1]), 0)
        pick = jnp.where(place == target, 1.0, 0.0).astype(jnp.bfloat16)
        part = lax.dot_general(
            pick, pair, (((1,), (1,)), ((), ())), preferred_element_type=jnp.float32
        )
        if n == 0:
            total[...] = part
        else:
            total[...] += part
    local = total[:, :128] + total[:, 128:]
    out_ref[0] = local
    place = lax.broadcasted_iota(jnp.int32, (cells, slots), 0)
    pick = jnp.where(place == cell_ref[...], 1.0, 0.0).astype(jnp.bfloat16)
    both = lax.dot_general(
        split(local, 1), pick, (((0,), (0,)), ((), ())), preferred_element_type=jnp.float32
    )
    far = jnp.sum((both[:128] + both[128:]) * basis_ref[...].astype(jnp.float32), axis=0, keepdims=True)
    slot = lax.broadcasted_iota(jnp.int32, (1, slots), 1)
    potential_ref[...] = jnp.where(slot < live_ref[0], near_ref[...] + far, 0.0)


def split(value, axis):
    high = value.astype(jnp.bfloat16)
    low = (value - high.astype(jnp.float32)).astype(jnp.bfloat16)
    return jnp.concatenate([high, low], axis=axis)


def translate(me, counts, table, lists, parts, cells, near, live, cell, basis):
    flat = [(a, b, relay, k) for a, (_, relay, ks) in enumerate(parts) for b, k in enumerate(ks)]
    groups = [flat[i : i + 4] for i in range(0, len(flat), 4)]
    return pl.pallas_call(
        functools.partial(translate_kernel, groups),
        out_shape=(
            jax.ShapeDtypeStruct((1, cells, 128), jnp.float32),
            jax.ShapeDtypeStruct(near.shape, jnp.float32),
        ),
        in_specs=[pl.BlockSpec(memory_space=pltpu.SMEM)] * 3
        + [pl.BlockSpec(memory_space=pltpu.VMEM)] * (5 + len(parts)),
        out_specs=[pl.BlockSpec(memory_space=pltpu.VMEM)] * 2,
        scratch_shapes=[pltpu.VMEM((cells, 256), jnp.float32)],
        compiler_params=pltpu.CompilerParams(vmem_limit_bytes=VMEM_BYTES),
        cost_estimate=pl.CostEstimate(
            flops=2 * len(flat) * 128 * 256 * (table.shape[1] + cells),
            bytes_accessed=len(flat) * 32768 + 2 * cells * 512,
            transcendentals=0,
        ),
    )(me, counts, live, table, lists, near, cell, basis, *[part for part, _, _ in parts])


def extended(block, axis):
    count = lax.axis_size(axis)
    forward = [(i, i + 1) for i in range(count - 1)]
    backward = [(target, source) for source, target in forward]
    return [lax.ppermute(block, axis, forward), block, lax.ppermute(block, axis, backward)]


def pair_sum(targets, sources):
    dist = (targets[0][:, None] - sources[0][None, :]) ** 2
    dist = dist + (targets[1][:, None] - sources[1][None, :]) ** 2
    dist = dist + (targets[2][:, None] - sources[2][None, :]) ** 2
    return jnp.sum(sources[3][None, :] / jnp.sqrt(dist + SOFT), axis=1)


def shards(
    multipoles,
    translations,
    m2l_list,
    send_counts,
    positions,
    charges,
    leaf_counts,
    particle_cell,
    basis,
):
    cells_dev = multipoles.shape[1]
    part_dev = charges.shape[1]
    me = lax.axis_index("slab").astype(jnp.int32).reshape(1)
    lists = m2l_list.reshape(3, SLABS, m2l_list.shape[2] // SLABS)
    counts = send_counts[0]

    ring = cells_dev // 32 * GATHERED
    groups = [list(range(i, SLABS, STRIDE)) for i in range(STRIDE)]
    gathered = lax.all_gather(multipoles[0, :ring], "slab", axis_index_groups=groups)
    rest = multipoles[0, ring:]

    asked = [shifted(value, relay) for value, relay in zip(ask(me, lists), RELAYED, strict=True)]

    chain = {0: rest}
    for k in (1, 2, 3):
        chain[-k] = shifted(chain[1 - k], STRIDE)
        chain[k] = shifted(chain[k - 1], -STRIDE)
    live = jnp.arange(part_dev, dtype=jnp.int32) < leaf_counts[0, 0]
    masked = jnp.where(live, charges[0], 0.0)
    stacked = jnp.concatenate([positions[0], masked[None, :]], axis=0)
    near = sum(pair_sum(positions[0], sources) for sources in extended(stacked, "grp"))
    near = jnp.where(live, near, 0.0)[None, :]
    table = split_table(translations)
    places = {k: [(i, False, ring)] for i, k in enumerate(EARLY)}
    early = pack(places, [chain[k] for k in EARLY], me, lists, asked)
    up, down, early, near, table = lax.optimization_barrier((chain[-3], chain[3], early, near, table))

    middle = rest.shape[0] // 2
    ends = [shifted(up[:middle], STRIDE), shifted(down[middle:], -STRIDE)]
    places = {k: [(0, True, 0)] for k in EARLY}
    places |= {3: [(0, True, 0), (1, False, ring)], -3: [(0, True, 0), (2, False, ring)]}
    places[4] = [(0, True, 0), (3, False, ring), (4, False, ring + middle)]
    packed = pack(places, [gathered, down, up, *ends], me, lists, asked, EARLY, early)
    parts = [(packed[0], 0, ORDER)]
    for value, (relay, ks) in zip(packed[1:], RELAYED.items(), strict=True):
        parts.append((shifted(value, -relay), relay, ks))
    return translate(
        me, counts, table, lists, parts, cells_dev, near, leaf_counts[0], particle_cell, basis[0]
    )


def solution(mesh):
    placed = (
        P("grp", "slab", None),
        P(),
        P(None, "grp", "slab"),
        P("grp", "slab"),
        P("grp", None, "slab"),
        P("grp", "slab"),
        P("grp", "slab"),
        P("grp", "slab"),
        P("grp", None, "slab"),
    )
    return jax.shard_map(
        shards,
        mesh=mesh,
        in_specs=placed,
        out_specs=(P("grp", "slab", None), P("grp", "slab")),
        check_vma=False,
    )
```

```python
import functools

import jax
import jax.numpy as jnp
from jax import lax
from jax.experimental import pallas as pl
from jax.experimental.pallas import tpu as pltpu
from jax.sharding import PartitionSpec as P

SOFT = 0.01
SLABS = 32
STRIDE = 4
EARLY = (0, 1, -1, 2, -2)
ORDER = (*EARLY, 3, -3, 4)
RELAYED = {1: ORDER, -1: ORDER, 2: (0, 1, 2, 3), -2: (0, -1, -2, -3)}
VMEM_BYTES = 56 * 1024 * 1024


def shifted(value, amount):
    count = lax.axis_size("slab")
    pairs = [(i, (i + amount) % count) for i in range(count)]
    return lax.ppermute(value, "slab", pairs)


def ask_kernel(me_ref, list_ref, *outs):
    for out, (relay, ks) in zip(outs, RELAYED.items(), strict=True):
        for i, k in enumerate(ks):
            out[pl.ds(i, 1), :] = list_ref[1, pl.ds(peer(me_ref[0], relay, k), 1), :]


def peer(me, relay, k):
    return lax.rem(me + (relay + STRIDE * k + SLABS), SLABS)


def ask(me, lists):
    return pl.pallas_call(
        ask_kernel,
        out_shape=[jax.ShapeDtypeStruct((len(ks), lists.shape[2]), jnp.int32) for ks in RELAYED.values()],
        in_specs=[pl.BlockSpec(memory_space=pltpu.SMEM), pl.BlockSpec(memory_space=pltpu.VMEM)],
        out_specs=[pl.BlockSpec(memory_space=pltpu.VMEM)] * len(RELAYED),
    )(me, lists)


def table_kernel(matrix_ref, out_ref):
    for o in range(matrix_ref.shape[0]):
        turned = matrix_ref[o].T
        high = turned.astype(jnp.bfloat16)
        out_ref[0:128, o * 128 : (o + 1) * 128] = high
        rest = turned - high.astype(jnp.float32)
        out_ref[128:256, o * 128 : (o + 1) * 128] = rest.astype(jnp.bfloat16)


def split_table(translations):
    return pl.pallas_call(
        table_kernel,
        out_shape=jax.ShapeDtypeStruct((256, translations.shape[0] * 128), jnp.bfloat16),
        in_specs=[pl.BlockSpec(memory_space=pltpu.VMEM)],
        out_specs=pl.BlockSpec(memory_space=pltpu.VMEM),
        compiler_params=pltpu.CompilerParams(vmem_limit_bytes=VMEM_BYTES),
    )(translations)


def pack_kernel(plan, known, me_ref, list_ref, *refs):
    asked = dict(zip(RELAYED, refs[: len(RELAYED)], strict=True))
    refs = refs[len(RELAYED) :]
    count = len(RELAYED) + 1
    before = refs[:count] if known else ()
    blocks, outs = refs[len(before) : -count], refs[-count:]
    for k, parts, uses in plan:
        if k in known:
            for relay, slot in uses:
                dest = 0 if relay == 0 else 1 + list(RELAYED).index(relay)
                outs[dest][slot] = before[dest][kept(known, relay).index(k)]
            continue
        lists = []
        for relay, _ in uses:
            if relay == 0:
                lists.append(list_ref[1, pl.ds(peer(me_ref[0], 0, k), 1), :])
            else:
                lists.append(asked[relay][pl.ds(RELAYED[relay].index(k), 1), :])
        wanted = jnp.concatenate(lists, axis=1)
        total = None
        for ref, base in parts:
            block = blocks[ref][...]
            place = lax.broadcasted_iota(jnp.int32, (block.shape[0], wanted.shape[1]), 0)
            pick = jnp.where(place + base == wanted, 1.0, 0.0).astype(jnp.bfloat16)
            part = lax.dot_general(
                block, pick, (((0,), (0,)), ((), ())), preferred_element_type=jnp.float32
            )
            total = part if total is None else total + part
        rows = total.astype(jnp.bfloat16)
        for i, (relay, slot) in enumerate(uses):
            dest = 0 if relay == 0 else 1 + list(RELAYED).index(relay)
            outs[dest][slot] = rows[:, i * 128 : (i + 1) * 128]


def kept(names, relay):
    return [k for k in names if relay == 0 or k in RELAYED[relay]]


def pack(parts, blocks, me, lists, asked, known=(), before=()):
    relays = [0, *RELAYED]
    plan = []
    for k in parts:
        uses = [(r, kept(parts, r).index(k)) for r in relays if r == 0 or k in RELAYED[r]]
        plan.append((k, parts[k], uses))
    sizes = [len(kept(parts, r)) for r in relays]
    return pl.pallas_call(
        functools.partial(pack_kernel, plan, known),
        out_shape=[jax.ShapeDtypeStruct((size, 128, 128), jnp.bfloat16) for size in sizes],
        in_specs=[pl.BlockSpec(memory_space=pltpu.SMEM)]
        + [pl.BlockSpec(memory_space=pltpu.VMEM)] * (1 + len(asked) + len(before) + len(blocks)),
        out_specs=[pl.BlockSpec(memory_space=pltpu.VMEM)] * len(sizes),
        compiler_params=pltpu.CompilerParams(vmem_limit_bytes=VMEM_BYTES),
        cost_estimate=pl.CostEstimate(
            flops=2 * 4096 * 512 * 128, bytes_accessed=2 * 1024 * 1024, transcendentals=0
        ),
    )(me, lists, *asked, *before, *blocks)


def translate_kernel(groups, me_ref, count_ref, live_ref, table_ref, list_ref, near_ref, cell_ref, basis_ref, *refs):
    rows, out_ref, potential_ref, total = refs[:-3], refs[-3], refs[-2], refs[-1]
    cells, slots = out_ref.shape[1], near_ref.shape[1]
    offsets = table_ref.shape[1] // 128
    lane = lax.broadcasted_iota(jnp.int32, (1, 128), 1)
    for n, group in enumerate(groups):
        taken = jnp.concatenate([rows[a][b] for a, b, _, _ in group], axis=1)
        targets, kinds = [], []
        for _, _, relay, k in group:
            at = peer(me_ref[0], relay, k)
            targets.append(list_ref[0, pl.ds(at, 1), :])
            kinds.append(jnp.where(lane < count_ref[at], list_ref[2, pl.ds(at, 1), :], -1))
        target = jnp.concatenate(targets, axis=1)
        kind = jnp.concatenate(kinds, axis=1)
        spread = jnp.concatenate(
            [taken * jnp.where(kind == o, 1.0, 0.0).astype(jnp.bfloat16) for o in range(offsets)],
            axis=0,
        )
        both = jnp.dot(table_ref[...], spread, preferred_element_type=jnp.float32)
        pair = split(both[:128] + both[128:], 0)
        place = lax.broadcasted_iota(jnp.int32, (cells, target.shape[1]), 0)
        pick = jnp.where(place == target, 1.0, 0.0).astype(jnp.bfloat16)
        part = lax.dot_general(
            pick, pair, (((1,), (1,)), ((), ())), preferred_element_type=jnp.float32
        )
        if n == 0:
            total[...] = part
        else:
            total[...] += part
    local = total[:, :128] + total[:, 128:]
    out_ref[0] = local
    place = lax.broadcasted_iota(jnp.int32, (cells, slots), 0)
    pick = jnp.where(place == cell_ref[...], 1.0, 0.0).astype(jnp.bfloat16)
    both = lax.dot_general(
        split(local, 1), pick, (((0,), (0,)), ((), ())), preferred_element_type=jnp.float32
    )
    far = jnp.sum((both[:128] + both[128:]) * basis_ref[...].astype(jnp.float32), axis=0, keepdims=True)
    slot = lax.broadcasted_iota(jnp.int32, (1, slots), 1)
    potential_ref[...] = jnp.where(slot < live_ref[0], near_ref[...] + far, 0.0)


def split(value, axis):
    high = value.astype(jnp.bfloat16)
    low = (value - high.astype(jnp.float32)).astype(jnp.bfloat16)
    return jnp.concatenate([high, low], axis=axis)


def translate(me, counts, table, lists, parts, cells, near, live, cell, basis):
    flat = [(a, b, relay, k) for a, (_, relay, ks) in enumerate(parts) for b, k in enumerate(ks)]
    groups = [flat[i : i + 4] for i in range(0, len(flat), 4)]
    return pl.pallas_call(
        functools.partial(translate_kernel, groups),
        out_shape=(
            jax.ShapeDtypeStruct((1, cells, 128), jnp.float32),
            jax.ShapeDtypeStruct(near.shape, jnp.float32),
        ),
        in_specs=[pl.BlockSpec(memory_space=pltpu.SMEM)] * 3
        + [pl.BlockSpec(memory_space=pltpu.VMEM)] * (5 + len(parts)),
        out_specs=[pl.BlockSpec(memory_space=pltpu.VMEM)] * 2,
        scratch_shapes=[pltpu.VMEM((cells, 256), jnp.float32)],
        compiler_params=pltpu.CompilerParams(vmem_limit_bytes=VMEM_BYTES),
        cost_estimate=pl.CostEstimate(
            flops=2 * len(flat) * 128 * 256 * (table.shape[1] + cells),
            bytes_accessed=len(flat) * 32768 + 2 * cells * 512,
            transcendentals=0,
        ),
    )(me, counts, live, table, lists, near, cell, basis, *[part for part, _, _ in parts])


def extended(block, axis):
    count = lax.axis_size(axis)
    forward = [(i, i + 1) for i in range(count - 1)]
    backward = [(target, source) for source, target in forward]
    return [lax.ppermute(block, axis, forward), block, lax.ppermute(block, axis, backward)]


def pair_sum(targets, sources):
    dist = (targets[0][:, None] - sources[0][None, :]) ** 2
    dist = dist + (targets[1][:, None] - sources[1][None, :]) ** 2
    dist = dist + (targets[2][:, None] - sources[2][None, :]) ** 2
    return jnp.sum(sources[3][None, :] / jnp.sqrt(dist + SOFT), axis=1)


def shards(
    multipoles,
    translations,
    m2l_list,
    send_counts,
    positions,
    charges,
    leaf_counts,
    particle_cell,
    basis,
):
    cells_dev = multipoles.shape[1]
    part_dev = charges.shape[1]
    me = lax.axis_index("slab").astype(jnp.int32).reshape(1)
    lists = m2l_list.reshape(3, SLABS, m2l_list.shape[2] // SLABS)
    counts = send_counts[0]

    asked = [shifted(value, relay) for value, relay in zip(ask(me, lists), RELAYED, strict=True)]

    chain = {0: multipoles[0]}
    for k in (1, 2, 3):
        chain[-k] = shifted(chain[1 - k], STRIDE)
        chain[k] = shifted(chain[k - 1], -STRIDE)
    live = jnp.arange(part_dev, dtype=jnp.int32) < leaf_counts[0, 0]
    masked = jnp.where(live, charges[0], 0.0)
    stacked = jnp.concatenate([positions[0], masked[None, :]], axis=0)
    near = sum(pair_sum(positions[0], sources) for sources in extended(stacked, "grp"))
    near = jnp.where(live, near, 0.0)[None, :]
    table = split_table(translations)
    early = pack({k: [(i, 0)] for i, k in enumerate(EARLY)}, [chain[k] for k in EARLY], me, lists, asked)
    up, down = chain[-3], chain[3]
    asked, early, near, table = lax.optimization_barrier((asked, early, near, table))

    middle = cells_dev // 2
    ends = [shifted(up[:middle], STRIDE), shifted(down[middle:], -STRIDE)]
    places = {k: [] for k in EARLY}
    places |= {3: [(0, 0)], -3: [(1, 0)], 4: [(2, 0), (3, middle)]}
    packed = pack(places, [down, up, *ends], me, lists, asked, EARLY, early)
    parts = [(packed[0], 0, ORDER)]
    for value, (relay, ks) in zip(packed[1:], RELAYED.items(), strict=True):
        parts.append((shifted(value, -relay), relay, ks))
    return translate(
        me, counts, table, lists, parts, cells_dev, near, leaf_counts[0], particle_cell, basis[0]
    )


def solution(mesh):
    placed = (
        P("grp", "slab", None),
        P(),
        P(None, "grp", "slab"),
        P("grp", "slab"),
        P("grp", None, "slab"),
        P("grp", "slab"),
        P("grp", "slab"),
        P("grp", "slab"),
        P("grp", None, "slab"),
    )
    return jax.shard_map(
        shards,
        mesh=mesh,
        in_specs=placed,
        out_specs=(P("grp", "slab", None), P("grp", "slab")),
        check_vma=False,
    )
```

```python
import functools

import jax
import jax.numpy as jnp
from jax import lax
from jax.experimental import pallas as pl
from jax.experimental.pallas import tpu as pltpu
from jax.sharding import PartitionSpec as P

SOFT = 0.01
SLABS = 32
STRIDE = 4
EARLY = (0, 1, -1, 2, -2, 3, -3)
LATE = (4,)
ORDER = EARLY + LATE
RELAYED = {1: ORDER, -1: ORDER, 2: (0, 1, 2, 3), -2: (0, -1, -2, -3)}
VMEM_BYTES = 56 * 1024 * 1024


def shifted(value, amount):
    count = lax.axis_size("slab")
    pairs = [(i, (i + amount) % count) for i in range(count)]
    return lax.ppermute(value, "slab", pairs)


def ask_kernel(me_ref, list_ref, *outs):
    for out, (relay, ks) in zip(outs, RELAYED.items(), strict=True):
        for i, k in enumerate(ks):
            out[pl.ds(i, 1), :] = list_ref[1, pl.ds(peer(me_ref[0], relay, k), 1), :]


def peer(me, relay, k):
    return lax.rem(me + (relay + STRIDE * k + SLABS), SLABS)


def ask(me, lists):
    return pl.pallas_call(
        ask_kernel,
        out_shape=[jax.ShapeDtypeStruct((len(ks), lists.shape[2]), jnp.int32) for ks in RELAYED.values()],
        in_specs=[pl.BlockSpec(memory_space=pltpu.SMEM), pl.BlockSpec(memory_space=pltpu.VMEM)],
        out_specs=[pl.BlockSpec(memory_space=pltpu.VMEM)] * len(RELAYED),
    )(me, lists)


def table_kernel(matrix_ref, out_ref):
    for o in range(matrix_ref.shape[0]):
        turned = matrix_ref[o].T
        high = turned.astype(jnp.bfloat16)
        out_ref[0:128, o * 128 : (o + 1) * 128] = high
        rest = turned - high.astype(jnp.float32)
        out_ref[128:256, o * 128 : (o + 1) * 128] = rest.astype(jnp.bfloat16)


def split_table(translations):
    return pl.pallas_call(
        table_kernel,
        out_shape=jax.ShapeDtypeStruct((256, translations.shape[0] * 128), jnp.bfloat16),
        in_specs=[pl.BlockSpec(memory_space=pltpu.VMEM)],
        out_specs=pl.BlockSpec(memory_space=pltpu.VMEM),
        compiler_params=pltpu.CompilerParams(vmem_limit_bytes=VMEM_BYTES),
    )(translations)


def pack_kernel(plan, known, me_ref, list_ref, *refs):
    asked = dict(zip(RELAYED, refs[: len(RELAYED)], strict=True))
    refs = refs[len(RELAYED) :]
    count = len(RELAYED) + 1
    before = refs[:count] if known else ()
    blocks, outs = refs[len(before) : -count], refs[-count:]
    for k, parts, uses in plan:
        if k in known:
            for relay, slot in uses:
                dest = 0 if relay == 0 else 1 + list(RELAYED).index(relay)
                outs[dest][slot] = before[dest][kept(known, relay).index(k)]
            continue
        lists = []
        for relay, _ in uses:
            if relay == 0:
                lists.append(list_ref[1, pl.ds(peer(me_ref[0], 0, k), 1), :])
            else:
                lists.append(asked[relay][pl.ds(RELAYED[relay].index(k), 1), :])
        wanted = jnp.concatenate(lists, axis=1)
        total = None
        for ref, base in parts:
            block = blocks[ref][...]
            place = lax.broadcasted_iota(jnp.int32, (block.shape[0], wanted.shape[1]), 0)
            pick = jnp.where(place + base == wanted, 1.0, 0.0).astype(jnp.bfloat16)
            part = lax.dot_general(
                block, pick, (((0,), (0,)), ((), ())), preferred_element_type=jnp.float32
            )
            total = part if total is None else total + part
        rows = total.astype(jnp.bfloat16)
        for i, (relay, slot) in enumerate(uses):
            dest = 0 if relay == 0 else 1 + list(RELAYED).index(relay)
            outs[dest][slot] = rows[:, i * 128 : (i + 1) * 128]


def kept(names, relay):
    return [k for k in names if relay == 0 or k in RELAYED[relay]]


def pack(parts, blocks, me, lists, asked, known=(), before=()):
    relays = [0, *RELAYED]
    plan = []
    for k in parts:
        uses = [(r, kept(parts, r).index(k)) for r in relays if r == 0 or k in RELAYED[r]]
        plan.append((k, parts[k], uses))
    sizes = [len(kept(parts, r)) for r in relays]
    return pl.pallas_call(
        functools.partial(pack_kernel, plan, known),
        out_shape=[jax.ShapeDtypeStruct((size, 128, 128), jnp.bfloat16) for size in sizes],
        in_specs=[pl.BlockSpec(memory_space=pltpu.SMEM)]
        + [pl.BlockSpec(memory_space=pltpu.VMEM)] * (1 + len(asked) + len(before) + len(blocks)),
        out_specs=[pl.BlockSpec(memory_space=pltpu.VMEM)] * len(sizes),
        compiler_params=pltpu.CompilerParams(vmem_limit_bytes=VMEM_BYTES),
        cost_estimate=pl.CostEstimate(
            flops=2 * 4096 * 512 * 128, bytes_accessed=2 * 1024 * 1024, transcendentals=0
        ),
    )(me, lists, *asked, *before, *blocks)


def translate_kernel(groups, me_ref, count_ref, table_ref, list_ref, rows, total):
    cells = total.shape[0]
    offsets = table_ref.shape[1] // 128
    lane = lax.broadcasted_iota(jnp.int32, (1, 128), 1)
    for n, group in enumerate(groups):
        taken = jnp.concatenate([rows[a][b] for a, b, _, _ in group], axis=1)
        targets, kinds = [], []
        for _, _, relay, k in group:
            at = peer(me_ref[0], relay, k)
            targets.append(list_ref[0, pl.ds(at, 1), :])
            kinds.append(jnp.where(lane < count_ref[at], list_ref[2, pl.ds(at, 1), :], -1))
        target = jnp.concatenate(targets, axis=1)
        kind = jnp.concatenate(kinds, axis=1)
        spread = jnp.concatenate(
            [taken * jnp.where(kind == o, 1.0, 0.0).astype(jnp.bfloat16) for o in range(offsets)],
            axis=0,
        )
        both = jnp.dot(table_ref[...], spread, preferred_element_type=jnp.float32)
        pair = split(both[:128] + both[128:], 0)
        place = lax.broadcasted_iota(jnp.int32, (cells, target.shape[1]), 0)
        pick = jnp.where(place == target, 1.0, 0.0).astype(jnp.bfloat16)
        part = lax.dot_general(
            pick, pair, (((1,), (1,)), ((), ())), preferred_element_type=jnp.float32
        )
        if n == 0:
            total[...] = part
        else:
            total[...] += part
    return total[:, :128] + total[:, 128:]


def first_kernel(groups, me_ref, count_ref, table_ref, list_ref, *refs):
    rows, out_ref, total = refs[:-2], refs[-2], refs[-1]
    out_ref[...] = translate_kernel(groups, me_ref, count_ref, table_ref, list_ref, rows, total)


def last_kernel(
    groups, me_ref, count_ref, live_ref, table_ref, list_ref, start_ref, near_ref, cell_ref, basis_ref, *refs
):
    rows, out_ref, potential_ref, total = refs[:-3], refs[-3], refs[-2], refs[-1]
    cells, slots = out_ref.shape[1], near_ref.shape[1]
    local = translate_kernel(groups, me_ref, count_ref, table_ref, list_ref, rows, total)
    local = local + start_ref[...]
    out_ref[0] = local
    place = lax.broadcasted_iota(jnp.int32, (cells, slots), 0)
    pick = jnp.where(place == cell_ref[...], 1.0, 0.0).astype(jnp.bfloat16)
    both = lax.dot_general(
        split(local, 1), pick, (((0,), (0,)), ((), ())), preferred_element_type=jnp.float32
    )
    far = jnp.sum((both[:128] + both[128:]) * basis_ref[...].astype(jnp.float32), axis=0, keepdims=True)
    slot = lax.broadcasted_iota(jnp.int32, (1, slots), 1)
    potential_ref[...] = jnp.where(slot < live_ref[0], near_ref[...] + far, 0.0)


def split(value, axis):
    high = value.astype(jnp.bfloat16)
    low = (value - high.astype(jnp.float32)).astype(jnp.bfloat16)
    return jnp.concatenate([high, low], axis=axis)


def translate(me, counts, table, lists, parts, cells, last=None):
    flat = [(a, b, relay, k) for a, (_, relay, ks) in enumerate(parts) for b, k in enumerate(ks)]
    groups = [flat[i : i + 4] for i in range(0, len(flat), 4)]
    if last is None:
        body, scalars, arrays = first_kernel, [me, counts], [table, lists]
        shapes = jax.ShapeDtypeStruct((cells, 128), jnp.float32)
        outs = pl.BlockSpec(memory_space=pltpu.VMEM)
    else:
        start, near, live, cell, basis = last
        body, scalars, arrays = last_kernel, [me, counts, live], [table, lists, start, near, cell, basis]
        shapes = [
            jax.ShapeDtypeStruct((1, cells, 128), jnp.float32),
            jax.ShapeDtypeStruct(near.shape, jnp.float32),
        ]
        outs = [pl.BlockSpec(memory_space=pltpu.VMEM)] * 2
    return pl.pallas_call(
        functools.partial(body, groups),
        out_shape=shapes,
        in_specs=[pl.BlockSpec(memory_space=pltpu.SMEM)] * len(scalars)
        + [pl.BlockSpec(memory_space=pltpu.VMEM)] * (len(arrays) + len(parts)),
        out_specs=outs,
        scratch_shapes=[pltpu.VMEM((cells, 256), jnp.float32)],
        compiler_params=pltpu.CompilerParams(vmem_limit_bytes=VMEM_BYTES),
        cost_estimate=pl.CostEstimate(
            flops=2 * len(flat) * 128 * 256 * (table.shape[1] + cells),
            bytes_accessed=len(flat) * 32768 + 2 * cells * 512,
            transcendentals=0,
        ),
    )(*scalars, *arrays, *[part for part, _, _ in parts])


def extended(block, axis):
    count = lax.axis_size(axis)
    forward = [(i, i + 1) for i in range(count - 1)]
    backward = [(target, source) for source, target in forward]
    return [lax.ppermute(block, axis, forward), block, lax.ppermute(block, axis, backward)]


def pair_sum(targets, sources):
    dist = (targets[0][:, None] - sources[0][None, :]) ** 2
    dist = dist + (targets[1][:, None] - sources[1][None, :]) ** 2
    dist = dist + (targets[2][:, None] - sources[2][None, :]) ** 2
    return jnp.sum(sources[3][None, :] / jnp.sqrt(dist + SOFT), axis=1)


def shards(
    multipoles,
    translations,
    m2l_list,
    send_counts,
    positions,
    charges,
    leaf_counts,
    particle_cell,
    basis,
):
    cells_dev = multipoles.shape[1]
    part_dev = charges.shape[1]
    me = lax.axis_index("slab").astype(jnp.int32).reshape(1)
    lists = m2l_list.reshape(3, SLABS, m2l_list.shape[2] // SLABS)
    counts = send_counts[0]

    asked = [shifted(value, relay) for value, relay in zip(ask(me, lists), RELAYED, strict=True)]

    middle = cells_dev // 2
    chain = {0: (multipoles[0],)}
    for k in (1, 2, 3):
        if k == 2:
            sides = {key: (chain[key][0][:middle], chain[key][0][middle:]) for key in (1 - k, k - 1)}
        else:
            sides = chain
        chain[-k] = tuple(shifted(part, STRIDE) for part in sides[1 - k])
        chain[k] = tuple(shifted(part, -STRIDE) for part in reversed(sides[k - 1]))[::-1]
    chain[4] = (shifted(chain[-3][0], STRIDE), shifted(chain[3][1], -STRIDE))

    live = jnp.arange(part_dev, dtype=jnp.int32) < leaf_counts[0, 0]
    masked = jnp.where(live, charges[0], 0.0)
    stacked = jnp.concatenate([positions[0], masked[None, :]], axis=0)
    near = sum(pair_sum(positions[0], sources) for sources in extended(stacked, "grp"))
    near = jnp.where(live, near, 0.0)[None, :]
    table = split_table(translations)
    def places(names):
        spots, flat = {}, []
        for k in names:
            spots[k] = []
            for part, base in zip(chain[k], (0, middle), strict=False):
                spots[k].append((len(flat), base))
                flat.append(part)
        return spots, flat

    early = pack(*places(EARLY), me, lists, asked)
    asked, early, near, table = lax.optimization_barrier((asked, early, near, table))
    spots, flat = places(LATE)
    packed = pack({k: [] for k in EARLY} | spots, flat, me, lists, asked, EARLY, early)
    parts = []
    for value, (relay, ks) in zip(packed[1:], RELAYED.items(), strict=True):
        parts.append((shifted(value, -relay), relay, ks))
    add = functools.partial(translate, me, counts, table, lists)
    start = add([(packed[0], 0, ORDER)], cells_dev)
    return add(parts, cells_dev, (start, near, leaf_counts[0], particle_cell, basis[0]))


def solution(mesh):
    placed = (
        P("grp", "slab", None),
        P(),
        P(None, "grp", "slab"),
        P("grp", "slab"),
        P("grp", None, "slab"),
        P("grp", "slab"),
        P("grp", "slab"),
        P("grp", "slab"),
        P("grp", None, "slab"),
    )
    return jax.shard_map(
        shards,
        mesh=mesh,
        in_specs=placed,
        out_specs=(P("grp", "slab", None), P("grp", "slab")),
        check_vma=False,
    )
```

```python
import functools

import jax
import jax.numpy as jnp
from jax import lax
from jax.experimental import pallas as pl
from jax.experimental.pallas import tpu as pltpu
from jax.sharding import PartitionSpec as P

SOFT = 0.01
SLABS = 32
STRIDE = 4
EARLY = (0, 1, -1, 2, -2, 3, -3)
LATE = (4,)
ORDER = EARLY + LATE
RELAYED = {2: (0, 1, 2, 3), -2: (0, -1, -2, -3), 1: ORDER, -1: ORDER}
VMEM_BYTES = 56 * 1024 * 1024


def shifted(value, amount):
    count = lax.axis_size("slab")
    pairs = [(i, (i + amount) % count) for i in range(count)]
    return lax.ppermute(value, "slab", pairs)


def ask_kernel(me_ref, list_ref, *outs):
    for out, (relay, ks) in zip(outs, RELAYED.items(), strict=True):
        for i, k in enumerate(ks):
            out[pl.ds(i, 1), :] = list_ref[1, pl.ds(peer(me_ref[0], relay, k), 1), :]


def peer(me, relay, k):
    return lax.rem(me + (relay + STRIDE * k + SLABS), SLABS)


def ask(me, lists):
    return pl.pallas_call(
        ask_kernel,
        out_shape=[jax.ShapeDtypeStruct((len(ks), lists.shape[2]), jnp.int32) for ks in RELAYED.values()],
        in_specs=[pl.BlockSpec(memory_space=pltpu.SMEM), pl.BlockSpec(memory_space=pltpu.VMEM)],
        out_specs=[pl.BlockSpec(memory_space=pltpu.VMEM)] * len(RELAYED),
    )(me, lists)


def table_kernel(matrix_ref, out_ref):
    for o in range(matrix_ref.shape[0]):
        turned = matrix_ref[o].T
        high = turned.astype(jnp.bfloat16)
        out_ref[0:128, o * 128 : (o + 1) * 128] = high
        rest = turned - high.astype(jnp.float32)
        out_ref[128:256, o * 128 : (o + 1) * 128] = rest.astype(jnp.bfloat16)


def split_table(translations):
    return pl.pallas_call(
        table_kernel,
        out_shape=jax.ShapeDtypeStruct((256, translations.shape[0] * 128), jnp.bfloat16),
        in_specs=[pl.BlockSpec(memory_space=pltpu.VMEM)],
        out_specs=pl.BlockSpec(memory_space=pltpu.VMEM),
        compiler_params=pltpu.CompilerParams(vmem_limit_bytes=VMEM_BYTES),
    )(translations)


def pack_kernel(plan, known, me_ref, list_ref, *refs):
    asked = dict(zip(RELAYED, refs[: len(RELAYED)], strict=True))
    refs = refs[len(RELAYED) :]
    count = len(RELAYED) + 1
    before = refs[:count] if known else ()
    blocks, outs = refs[len(before) : -count], refs[-count:]
    for k, parts, uses in plan:
        if k in known:
            for relay, slot in uses:
                dest = 0 if relay == 0 else 1 + list(RELAYED).index(relay)
                outs[dest][slot] = before[dest][kept(known, relay).index(k)]
            continue
        lists = []
        for relay, _ in uses:
            if relay == 0:
                lists.append(list_ref[1, pl.ds(peer(me_ref[0], 0, k), 1), :])
            else:
                lists.append(asked[relay][pl.ds(RELAYED[relay].index(k), 1), :])
        wanted = jnp.concatenate(lists, axis=1)
        total = None
        for ref, base in parts:
            block = blocks[ref][...]
            place = lax.broadcasted_iota(jnp.int32, (block.shape[0], wanted.shape[1]), 0)
            pick = jnp.where(place + base == wanted, 1.0, 0.0).astype(jnp.bfloat16)
            part = lax.dot_general(
                block, pick, (((0,), (0,)), ((), ())), preferred_element_type=jnp.float32
            )
            total = part if total is None else total + part
        rows = total.astype(jnp.bfloat16)
        for i, (relay, slot) in enumerate(uses):
            dest = 0 if relay == 0 else 1 + list(RELAYED).index(relay)
            outs[dest][slot] = rows[:, i * 128 : (i + 1) * 128]


def kept(names, relay):
    return [k for k in names if relay == 0 or k in RELAYED[relay]]


def pack(parts, blocks, me, lists, asked, known=(), before=()):
    relays = [0, *RELAYED]
    plan = []
    for k in parts:
        uses = [(r, kept(parts, r).index(k)) for r in relays if r == 0 or k in RELAYED[r]]
        plan.append((k, parts[k], uses))
    sizes = [len(kept(parts, r)) for r in relays]
    return pl.pallas_call(
        functools.partial(pack_kernel, plan, known),
        out_shape=[jax.ShapeDtypeStruct((size, 128, 128), jnp.bfloat16) for size in sizes],
        in_specs=[pl.BlockSpec(memory_space=pltpu.SMEM)]
        + [pl.BlockSpec(memory_space=pltpu.VMEM)] * (1 + len(asked) + len(before) + len(blocks)),
        out_specs=[pl.BlockSpec(memory_space=pltpu.VMEM)] * len(sizes),
        compiler_params=pltpu.CompilerParams(vmem_limit_bytes=VMEM_BYTES),
        cost_estimate=pl.CostEstimate(
            flops=2 * 4096 * 512 * 128, bytes_accessed=2 * 1024 * 1024, transcendentals=0
        ),
    )(me, lists, *asked, *before, *blocks)


def translate_kernel(groups, me_ref, count_ref, table_ref, list_ref, rows, total):
    cells = total.shape[0]
    offsets = table_ref.shape[1] // 128
    lane = lax.broadcasted_iota(jnp.int32, (1, 128), 1)
    for n, group in enumerate(groups):
        taken = jnp.concatenate([rows[a][b] for a, b, _, _ in group], axis=1)
        targets, kinds = [], []
        for _, _, relay, k in group:
            at = peer(me_ref[0], relay, k)
            targets.append(list_ref[0, pl.ds(at, 1), :])
            kinds.append(jnp.where(lane < count_ref[at], list_ref[2, pl.ds(at, 1), :], -1))
        target = jnp.concatenate(targets, axis=1)
        kind = jnp.concatenate(kinds, axis=1)
        spread = jnp.concatenate(
            [taken * jnp.where(kind == o, 1.0, 0.0).astype(jnp.bfloat16) for o in range(offsets)],
            axis=0,
        )
        both = jnp.dot(table_ref[...], spread, preferred_element_type=jnp.float32)
        pair = split(both[:128] + both[128:], 0)
        place = lax.broadcasted_iota(jnp.int32, (cells, target.shape[1]), 0)
        pick = jnp.where(place == target, 1.0, 0.0).astype(jnp.bfloat16)
        part = lax.dot_general(
            pick, pair, (((1,), (1,)), ((), ())), preferred_element_type=jnp.float32
        )
        if n == 0:
            total[...] = part
        else:
            total[...] += part
    return total[:, :128] + total[:, 128:]


def first_kernel(groups, me_ref, count_ref, table_ref, list_ref, *refs):
    rows, out_ref, total = refs[:-2], refs[-2], refs[-1]
    out_ref[...] = translate_kernel(groups, me_ref, count_ref, table_ref, list_ref, rows, total)


def last_kernel(
    groups, me_ref, count_ref, live_ref, table_ref, list_ref, start_ref, near_ref, cell_ref, basis_ref, *refs
):
    rows, out_ref, potential_ref, total = refs[:-3], refs[-3], refs[-2], refs[-1]
    cells, slots = out_ref.shape[1], near_ref.shape[1]
    local = translate_kernel(groups, me_ref, count_ref, table_ref, list_ref, rows, total)
    local = local + start_ref[...]
    out_ref[0] = local
    place = lax.broadcasted_iota(jnp.int32, (cells, slots), 0)
    pick = jnp.where(place == cell_ref[...], 1.0, 0.0).astype(jnp.bfloat16)
    both = lax.dot_general(
        split(local, 1), pick, (((0,), (0,)), ((), ())), preferred_element_type=jnp.float32
    )
    far = jnp.sum((both[:128] + both[128:]) * basis_ref[...].astype(jnp.float32), axis=0, keepdims=True)
    slot = lax.broadcasted_iota(jnp.int32, (1, slots), 1)
    potential_ref[...] = jnp.where(slot < live_ref[0], near_ref[...] + far, 0.0)


def split(value, axis):
    high = value.astype(jnp.bfloat16)
    low = (value - high.astype(jnp.float32)).astype(jnp.bfloat16)
    return jnp.concatenate([high, low], axis=axis)


def translate(me, counts, table, lists, parts, cells, last=None):
    flat = [(a, b, relay, k) for a, (_, relay, ks) in enumerate(parts) for b, k in enumerate(ks)]
    groups = [flat[i : i + 4] for i in range(0, len(flat), 4)]
    if last is None:
        body, scalars, arrays = first_kernel, [me, counts], [table, lists]
        shapes = jax.ShapeDtypeStruct((cells, 128), jnp.float32)
        outs = pl.BlockSpec(memory_space=pltpu.VMEM)
    else:
        start, near, live, cell, basis = last
        body, scalars, arrays = last_kernel, [me, counts, live], [table, lists, start, near, cell, basis]
        shapes = [
            jax.ShapeDtypeStruct((1, cells, 128), jnp.float32),
            jax.ShapeDtypeStruct(near.shape, jnp.float32),
        ]
        outs = [pl.BlockSpec(memory_space=pltpu.VMEM)] * 2
    return pl.pallas_call(
        functools.partial(body, groups),
        out_shape=shapes,
        in_specs=[pl.BlockSpec(memory_space=pltpu.SMEM)] * len(scalars)
        + [pl.BlockSpec(memory_space=pltpu.VMEM)] * (len(arrays) + len(parts)),
        out_specs=outs,
        scratch_shapes=[pltpu.VMEM((cells, 256), jnp.float32)],
        compiler_params=pltpu.CompilerParams(vmem_limit_bytes=VMEM_BYTES),
        cost_estimate=pl.CostEstimate(
            flops=2 * len(flat) * 128 * 256 * (table.shape[1] + cells),
            bytes_accessed=len(flat) * 32768 + 2 * cells * 512,
            transcendentals=0,
        ),
    )(*scalars, *arrays, *[part for part, _, _ in parts])


def extended(block, axis):
    count = lax.axis_size(axis)
    forward = [(i, i + 1) for i in range(count - 1)]
    backward = [(target, source) for source, target in forward]
    return [lax.ppermute(block, axis, forward), block, lax.ppermute(block, axis, backward)]


def pair_sum(targets, sources):
    dist = (targets[0][:, None] - sources[0][None, :]) ** 2
    dist = dist + (targets[1][:, None] - sources[1][None, :]) ** 2
    dist = dist + (targets[2][:, None] - sources[2][None, :]) ** 2
    return jnp.sum(sources[3][None, :] / jnp.sqrt(dist + SOFT), axis=1)


def shards(
    multipoles,
    translations,
    m2l_list,
    send_counts,
    positions,
    charges,
    leaf_counts,
    particle_cell,
    basis,
):
    cells_dev = multipoles.shape[1]
    part_dev = charges.shape[1]
    me = lax.axis_index("slab").astype(jnp.int32).reshape(1)
    lists = m2l_list.reshape(3, SLABS, m2l_list.shape[2] // SLABS)
    counts = send_counts[0]

    asked = [shifted(value, relay) for value, relay in zip(ask(me, lists), RELAYED, strict=True)]

    middle = cells_dev // 2
    chain = {0: (multipoles[0],)}
    for k in (1, 2, 3):
        if k == 2:
            sides = {key: (chain[key][0][:middle], chain[key][0][middle:]) for key in (1 - k, k - 1)}
        else:
            sides = chain
        chain[-k] = tuple(shifted(part, STRIDE) for part in sides[1 - k])
        chain[k] = tuple(shifted(part, -STRIDE) for part in reversed(sides[k - 1]))[::-1]
    chain[4] = (shifted(chain[-3][0], STRIDE), shifted(chain[3][1], -STRIDE))

    live = jnp.arange(part_dev, dtype=jnp.int32) < leaf_counts[0, 0]
    masked = jnp.where(live, charges[0], 0.0)
    stacked = jnp.concatenate([positions[0], masked[None, :]], axis=0)
    near = sum(pair_sum(positions[0], sources) for sources in extended(stacked, "grp"))
    near = jnp.where(live, near, 0.0)[None, :]
    table = split_table(translations)
    def places(names):
        spots, flat = {}, []
        for k in names:
            spots[k] = []
            for part, base in zip(chain[k], (0, middle), strict=False):
                spots[k].append((len(flat), base))
                flat.append(part)
        return spots, flat

    early = pack(*places(EARLY), me, lists, asked)
    asked, early, near, table = lax.optimization_barrier((asked, early, near, table))
    spots, flat = places(LATE)
    packed = pack({k: [] for k in EARLY} | spots, flat, me, lists, asked, EARLY, early)
    parts = []
    for value, (relay, ks) in zip(packed[1:], RELAYED.items(), strict=True):
        parts.append((shifted(value, -relay), relay, ks))
    add = functools.partial(translate, me, counts, table, lists)
    start = add([(packed[0], 0, ORDER)], cells_dev)
    return add(parts, cells_dev, (start, near, leaf_counts[0], particle_cell, basis[0]))


def solution(mesh):
    placed = (
        P("grp", "slab", None),
        P(),
        P(None, "grp", "slab"),
        P("grp", "slab"),
        P("grp", None, "slab"),
        P("grp", "slab"),
        P("grp", "slab"),
        P("grp", "slab"),
        P("grp", None, "slab"),
    )
    return jax.shard_map(
        shards,
        mesh=mesh,
        in_specs=placed,
        out_specs=(P("grp", "slab", None), P("grp", "slab")),
        check_vma=False,
    )
```
